32 devices in a mesh: groups: 2 (over x), rows: 2 (over core), tensor: 8 (over z, y).
Axes of the slice: x: 2, y: 2, z: 4, core: 2. Of those that a mesh axis runs over, the one named last changes fastest.
Arguments:
- features: bfloat16 [6144, 8192], P(('groups', 'rows'), 'tensor'), parts along dimension 0, may hold values from -6 to 6
- qkv_weight: bfloat16 [8192, 10240], P(None, 'tensor'), may hold values from -0.0625 to 0.0625
- adapter_ids: int32 [6144, 1], P(('groups', 'rows')), parts along dimension 0, may hold values from 0 to 31; in each aligned block of 192 rows (0 to 191, 192 to 383, ...) at most 12 rows name the same one
- owner_slot: int32 [32], replicated, may hold values from 0 to 31, each once
- shrink_panels: bfloat16 [32, 8192, 64], P(('rows', 'tensor')), may hold values from -0.0625 to 0.0625
- expand_panels: bfloat16 [32, 64, 10240], P(('rows', 'tensor')), may hold values from -0.75 to 0.75
Outputs:
- projected: bfloat16 [6144, 10240], P(('groups', 'rows'), 'tensor'), parts along dimension 0
The draws below stay inside these ranges and needn't reach their ends.
There are 2 independent parts, one for each index of `groups`. The reference program is written for one: setup_inputs(seed, part) draws one part's arguments, and reference() takes and returns one part's arrays. A program takes and returns all parts, laid end to end along the dimension named above; an argument that names none is the same for every part. Nothing has to cross between parts.
Inputs may be any that keep to these rules, and one draw needn't show every extreme that they name: `adapter_ids`: each row names one adapter. In each aligned block of 192 rows no adapter is named by more than 12 rows, and in some block one adapter is named by exactly 12 rows. A permutation: the panels of adapter k stand at index owner_slot[k] of shrink_panels and expand_panels.
All inputs are finite; a program needn't handle non-finite values.
Results may differ from the reference program's by a relative error of at most 0.005.
Values may be sent and summed in bfloat16 or wider, within the bound.
A program may use at most 192 MiB of HBM per device.

```python
import math
import jax
import jax.numpy as jnp
import numpy as np
from jax import lax

D = 8192
E = 10240
R = 64
ADAPTERS = 32
TOKENS = 3072
BLOCK = 192
MOST = 12


def levels(own_key, extent, pieces, low, top_value):
    def one(position, blocks):
        draws = jax.random.uniform(jax.random.fold_in(jax.random.fold_in(own_key, 6), position), (blocks,), jnp.float32, low / len(pieces), top_value / len(pieces))
        return jnp.repeat(jnp.exp(draws), extent[position] // blocks).reshape((-1,) + (1,) * (len(extent) - position - 1))

    factor_of = one(*pieces[0])
    for cut in pieces[1:]:
        factor_of = factor_of * one(*cut)
    return factor_of


def assign_block(stream_key, own, number, rows, number_of, top, bound, lean):
    sequence = jax.random.permutation(stream_key, number_of)
    crowded, usual = load_shares(number_of, rows * top, bound, lean, True), load_shares(number_of, rows * top, bound, lean, False)
    places = jnp.arange(number_of)

    def named(tallies, offset_by):
        used = int((tallies > 0).sum())
        fixed = max(1, used // 4)
        moved = fixed + (places - fixed + offset_by * (used - fixed)) % max(1, number_of - fixed)
        return jnp.zeros((number_of,), jnp.int32).at[sequence[jnp.where(places < fixed, places, moved)]].set(jnp.asarray(tallies, jnp.int32))

    tallies = jnp.where(number % 4 == 0, named(crowded, number // 4), named(usual, number - number // 4 - 1))
    mixed = jax.random.permutation(jax.random.fold_in(own, 3), number_of)
    donor, sink = mixed[0:number_of // 2 * 2:2], mixed[1:number_of // 2 * 2:2]
    margin = jnp.minimum(tallies[donor] - 1, bound - tallies[sink]) // 2
    margin = jnp.where((donor == sequence[0]) | (sink == sequence[0]) | (tallies[sink] == 0), 0, jnp.maximum(margin, 0))
    moved = jax.random.randint(jax.random.fold_in(own, 4), (number_of // 2,), 0, 1 << 20) % (margin + 1)
    tallies = tallies.at[donor].add(-moved).at[sink].add(moved)
    members = jnp.searchsorted(jnp.cumsum(tallies), jnp.arange(rows * top), side="right").astype(jnp.int32)
    table = members.reshape(top, rows).T
    table = table[jax.random.permutation(jax.random.fold_in(own, 1), rows)]
    offset_by = jax.random.randint(jax.random.fold_in(own, 2), (rows, 1), 0, top)
    return jnp.take_along_axis(table, (jnp.arange(top)[None, :] + offset_by) % top, axis=1)


def load_shares(number_of, total, limit, slope, full):
    portions = [(1 << 20) // math.isqrt(standing ** slope) + 1 for standing in range(1, number_of + 1)]
    largest = limit if full else min(limit, max(-(-total // number_of), total * portions[0] // sum(portions)))
    least = 1 if total - largest >= number_of - 1 else 0
    given, spare = [largest] + [least] * (number_of - 1), total - largest - least * (number_of - 1)
    while spare > 0:
        movable = [i for i in range(1, number_of) if given[i] < largest] or [i for i in range(1, number_of) if given[i] < limit]
        pool, left = sum([portions[i] for i in movable]), spare
        for i in movable:
            extra = min(limit - given[i], max(1, left * portions[i] // pool), spare)
            given[i] = given[i] + extra
            spare = spare - extra
    return np.array(given)


def centred(own_key, shape, scale, bound, shards=(), dtype=jnp.bfloat16):
    loudness = levels(own_key, shape, shards, -0.22, 0.18) if shards else 1.0
    drawn = jax.random.normal(own_key, shape, jnp.float32) * scale * loudness
    return jnp.minimum(jnp.maximum(drawn, -bound), bound).astype(dtype)


def setup_inputs(seed: int = 0, part: int = 0) -> dict:
    streams_of = jax.random.split(jax.random.key(seed), 7)
    part_keys = jax.random.split(jax.random.fold_in(streams_of[6], part), 7)
    features = centred(part_keys[0], (TOKENS, D), 1.0, 6.0, ((0, 2), (1, 8)))
    qkv_weight = centred(streams_of[1], (D, E), D ** -0.5, 0.0625, ((1, 8),))
    adapter_ids_keys = jax.random.split(jax.random.fold_in(part_keys[2], 1), TOKENS // BLOCK)
    adapter_ids_turns = jax.random.permutation(jax.random.fold_in(part_keys[2], 3), TOKENS // BLOCK)
    adapter_ids = jax.vmap(lambda own, number: assign_block(jax.random.fold_in(part_keys[2], 2), own, number, BLOCK, ADAPTERS, 1, MOST, 2))(adapter_ids_keys, adapter_ids_turns).reshape((TOKENS, 1))
    owner_slot = jax.random.permutation(streams_of[3], ADAPTERS).astype(jnp.int32)
    shrink_panels = centred(streams_of[4], (ADAPTERS, D, R), D ** -0.5, 0.0625, ((0, 16),))
    expand_panels = centred(streams_of[5], (ADAPTERS, R, E), R ** -0.5, 0.75, ((0, 16),))
    return dict(features=features, qkv_weight=qkv_weight, adapter_ids=adapter_ids, owner_slot=owner_slot, shrink_panels=shrink_panels, expand_panels=expand_panels)


def reference(features, qkv_weight, adapter_ids, owner_slot, shrink_panels, expand_panels):
    base = jnp.dot(features, qkv_weight, preferred_element_type=jnp.float32)
    slot = owner_slot[adapter_ids[:, 0]].astype(jnp.int32)
    rows_total = features.shape[0]
    block_slots = slot.reshape(rows_total // 32, 32)
    block_rows = features.reshape(rows_total // 32, 32, features.shape[1])

    def one_block(pair):
        slots, rows = pair
        first = shrink_panels[slots].astype(jnp.float32)
        shrunk = jnp.einsum("id,idr->ir", rows.astype(jnp.float32), first).astype(jnp.bfloat16)
        second = expand_panels[slots].astype(jnp.float32)
        return jnp.einsum("ir,ire->ie", shrunk.astype(jnp.float32), second).astype(jnp.bfloat16)

    delta = lax.map(one_block, (block_slots, block_rows)).reshape(rows_total, qkv_weight.shape[1])
    return (base + delta.astype(jnp.float32)).astype(jnp.bfloat16)
```

```python
import functools

import jax
import jax.numpy as jnp
from jax import lax
from jax.experimental import pallas as pl
from jax.experimental.pallas import tpu as pltpu
from jax.sharding import PartitionSpec as P

CHUNKS = 8
LAG = 2


def slot_of(row_ids, owner_slot):
    count = owner_slot.shape[0]
    match = row_ids[:, None] == jnp.arange(count, dtype=jnp.int32)[None, :]
    return jnp.sum(jnp.where(match, owner_slot[None, :], 0), axis=1)


def gather_kernel(
    Z, Y, CH, NB,
    x_ref, w_ref, sh_ref, base_ref, low_ref,
    g, w, ws, acc, low,
    own_sem, w_sem, ws_sem, ws_send, ws_recv,
    up_send, dn_send, z_recv, ub_send, db_send, b_recv, y_send, y_recv, out_sem,
):
    NC = x_ref.shape[0] // CH
    DK = x_ref.shape[1]
    T = Z * Y
    NA = CH - NB
    t = lax.axis_index("tensor")
    r = lax.axis_index("rows")
    z, y = t // Y, lax.rem(t, Y)
    has_up, has_dn = z < Z - 1, z > 0
    up, dn, side = {"tensor": t + Y}, {"tensor": t - Y}, {"tensor": z * Y + (1 - y)}
    twin = {"rows": 1 - r}

    barrier = pltpu.get_barrier_semaphore()

    @pl.when(has_up)
    def _():
        pl.semaphore_signal(barrier, inc=1, device_id=up)

    @pl.when(has_dn)
    def _():
        pl.semaphore_signal(barrier, inc=1, device_id=dn)

    if Y == 2:
        pl.semaphore_signal(barrier, inc=1, device_id=side)
    pl.semaphore_signal(barrier, inc=1, device_id=twin)
    pl.semaphore_wait(barrier, has_up.astype(jnp.int32) + has_dn.astype(jnp.int32) + Y)

    own_copy = pltpu.make_async_copy(x_ref, g.at[t], own_sem)
    w_copy = pltpu.make_async_copy(w_ref, w, w_sem)
    ws_cols = pl.ds(pl.multiple_of(r * 128, 128), 128)
    ws_copy = pltpu.make_async_copy(sh_ref, ws.at[:, ws_cols], ws_sem)
    ws_remote = pltpu.make_async_remote_copy(
        src_ref=sh_ref, dst_ref=ws.at[:, ws_cols], send_sem=ws_send, recv_sem=ws_recv, device_id=twin,
    )
    twin_cols = pl.ds(pl.multiple_of((1 - r) * 128, 128), 128)
    ws_in = pltpu.make_async_remote_copy(
        src_ref=sh_ref, dst_ref=ws.at[:, twin_cols], send_sem=ws_send, recv_sem=ws_recv, device_id=twin,
    )

    def rows_all(c):
        return pl.ds(pl.multiple_of(c * CH, CH), CH)

    def rows_a(c):
        return pl.ds(pl.multiple_of(c * CH, 16), NA)

    def rows_b(c):
        return pl.ds(pl.multiple_of(c * CH + NA, 16), NB)

    def place(zs, ys, rows):
        return g.at[zs * Y + ys, rows]

    def own_src(c):
        return x_ref.at[rows_all(c)]

    def along(c, zs, src, upward):
        return pltpu.make_async_remote_copy(
            src_ref=src, dst_ref=place(zs, y, rows_all(c)),
            send_sem=(up_send if upward else dn_send).at[c, zs], recv_sem=z_recv.at[c, zs],
            device_id=up if upward else dn,
        )

    def along_b(c, zs, upward):
        ref = place(zs, 1 - y, rows_b(c))
        return pltpu.make_async_remote_copy(
            src_ref=ref, dst_ref=ref,
            send_sem=(ub_send if upward else db_send).at[c, zs], recv_sem=b_recv.at[c, zs],
            device_id=up if upward else dn,
        )

    def across_own(c):
        return pltpu.make_async_remote_copy(
            src_ref=own_src(c), dst_ref=place(z, y, rows_all(c)),
            send_sem=y_send.at[c, z], recv_sem=y_recv.at[c, z], device_id=side,
        )

    def across(c, zs):
        ref = place(zs, y, rows_a(c))
        return pltpu.make_async_remote_copy(
            src_ref=ref, dst_ref=ref,
            send_sem=y_send.at[c, zs], recv_sem=y_recv.at[c, zs], device_id=side,
        )

    def wait_into(ref, sem):
        pltpu.make_async_remote_copy(
            src_ref=ref, dst_ref=ref, send_sem=sem, recv_sem=sem, device_id=twin,
        ).wait_recv()

    def when_chunk(c, cond=True):
        return pl.when((c >= 0) & (c < NC) & cond)

    def out_copies(c):
        slot = lax.rem(c, 2)
        return (
            pltpu.make_async_copy(acc.at[slot], base_ref.at[rows_all(c)], out_sem.at[slot, 0]),
            pltpu.make_async_copy(low.at[slot], low_ref.at[rows_all(c)], out_sem.at[slot, 1]),
        )

    def compute(c):
        slot = lax.rem(c, 2)

        @pl.when(c >= 2)
        def _():
            for copy in out_copies(c - 2):
                copy.wait()

        def one(s, sums):
            rows = g[s, rows_all(c), :]
            depth = pl.ds(pl.multiple_of(s * DK, DK), DK)
            part = jnp.dot(rows, w[depth, :], preferred_element_type=jnp.float32)
            first = s == 0
            acc[slot] = jnp.where(first, part, acc[slot] + part)
            return sums + jnp.dot(rows, ws[depth, :], preferred_element_type=jnp.float32)

        sums = lax.fori_loop(0, T, one, jnp.zeros((CH, 256), jnp.float32))
        low[slot] = sums.astype(low.dtype)
        for copy in out_copies(c):
            copy.start()

    def step(k, carry):
        @pl.when(k < NC)
        def _():
            @pl.when(has_up)
            def _():
                along(k, z, own_src(k), True).start()

            @pl.when(has_dn)
            def _():
                along(k, z, own_src(k), False).start()

            if Y == 2:
                across_own(k).start()

        @pl.when(k == 0)
        def _():
            ws_remote.start()
            ws_copy.start()
            own_copy.start()
            w_copy.start()

        if Y == 2:
            c1 = k - LAG

            @when_chunk(c1)
            def _():
                wait_into(place(z, 1 - y, rows_all(c1)), y_recv.at[c1, z])

                @pl.when(has_up)
                def _():
                    along_b(c1, z, True).start()

                @pl.when(has_dn)
                def _():
                    along_b(c1, z, False).start()

        for d in range(1, Z):
            for upward in (True, False):
                zs = z - d if upward else z + d
                here = zs >= 0 if upward else zs < Z
                more = has_up if upward else has_dn
                c = k - LAG * d

                @when_chunk(c, here)
                def _(c=c, zs=zs, upward=upward, more=more):
                    ref = place(zs, y, rows_all(c))
                    wait_into(ref, z_recv.at[c, zs])

                    @pl.when(more)
                    def _():
                        along(c, zs, ref, upward).start()

                    if Y == 2:
                        across(c, zs).start()

                if Y == 2:
                    cb = k - LAG * (d + 1)

                    @when_chunk(cb, here)
                    def _(c=cb, zs=zs, upward=upward, more=more):
                        wait_into(place(zs, 1 - y, rows_b(c)), b_recv.at[c, zs])

                        @pl.when(more)
                        def _():
                            along_b(c, zs, upward).start()

        @pl.when(k == LAG * Z)
        def _():
            own_copy.wait()
            w_copy.wait()
            ws_copy.wait()
            ws_in.wait_recv()

        cc = k - LAG * Z

        @when_chunk(cc)
        def _():
            if Y == 2:
                for zs in range(Z):
                    @pl.when(zs != z)
                    def _(zs=zs):
                        wait_into(place(zs, 1 - y, rows_a(cc)), y_recv.at[cc, zs])
            compute(cc)

        return carry

    lax.fori_loop(0, NC + LAG * Z, step, 0)

    for c in range(NC - 2, NC):
        for copy in out_copies(c):
            copy.wait()

    ws_remote.wait_send()

    def drain(c, carry):
        for zs in range(Z):
            ref = place(zs, y, rows_all(c))

            @pl.when(has_up & (zs <= z))
            def _(zs=zs, ref=ref):
                along(c, zs, ref, True).wait_send()
                if Y == 2:
                    along_b(c, zs, True).wait_send()

            @pl.when(has_dn & (zs >= z))
            def _(zs=zs, ref=ref):
                along(c, zs, ref, False).wait_send()
                if Y == 2:
                    along_b(c, zs, False).wait_send()

            if Y == 2:
                @pl.when(zs == z)
                def _():
                    across_own(c).wait_send()

                @pl.when(zs != z)
                def _(zs=zs):
                    across(c, zs).wait_send()
        return carry

    lax.fori_loop(0, NC, drain, 0)


def gather_and_multiply(features, weight, shrink_flat, Z, Y):
    rows, depth = features.shape
    width, columns = weight.shape
    T = Z * Y
    CH = rows // CHUNKS
    NB = CH // 6 // 16 * 16
    DMA = pltpu.SemaphoreType.DMA
    per = (CHUNKS, Z)
    few = per if Y == 2 else (1, 1)
    return pl.pallas_call(
        functools.partial(gather_kernel, Z, Y, CH, NB),
        out_shape=(
            jax.ShapeDtypeStruct((rows, columns), jnp.float32),
            jax.ShapeDtypeStruct((rows, 256), jnp.bfloat16),
        ),
        in_specs=[pl.BlockSpec(memory_space=pl.ANY)] * 3,
        out_specs=[pl.BlockSpec(memory_space=pl.ANY)] * 2,
        scratch_shapes=[
            pltpu.VMEM((T, rows, depth), jnp.bfloat16),
            pltpu.VMEM((width, columns), jnp.bfloat16),
            pltpu.VMEM((width, 256), jnp.bfloat16),
            pltpu.VMEM((2, CH, columns), jnp.float32),
            pltpu.VMEM((2, CH, 256), jnp.bfloat16),
            DMA, DMA, DMA, DMA, DMA,
            DMA(per), DMA(per), DMA(per), DMA(few), DMA(few), DMA(few), DMA(few), DMA(few),
            DMA((2, 2)),
        ],
        compiler_params=pltpu.CompilerParams(
            collective_id=0, has_side_effects=True, vmem_limit_bytes=62 * 1024 * 1024,
        ),
        cost_estimate=pl.CostEstimate(
            flops=2 * rows * width * (columns + 256), bytes_accessed=200_000_000, transcendentals=0,
        ),
    )(features, weight, shrink_flat)


def on_device(Z, Y, features, qkv_weight, adapter_ids, owner_slot, shrink_panels, expand_panels):
    rows = features.shape[0]
    columns = qkv_weight.shape[1]
    T = Z * Y
    per_device, width, rank = shrink_panels.shape
    adapter_count = owner_slot.shape[0]
    G = lax.axis_size("groups")
    t = lax.axis_index("tensor")
    slot = slot_of(adapter_ids[:, 0], owner_slot)

    share = rank // G
    mine = lax.dynamic_slice_in_dim(expand_panels, lax.axis_index("groups") * share, share, 1)
    mine = mine.reshape(per_device, share, T, columns).transpose(2, 0, 1, 3)
    got = lax.all_to_all(mine, "tensor", split_axis=0, concat_axis=0, tiled=True)
    panels = lax.all_gather(got, ("rows", "groups"), axis=0, tiled=False)
    panels = panels.reshape(2, G, T, per_device, share, columns).transpose(0, 2, 3, 1, 4, 5)
    panels = panels.reshape(adapter_count * rank, columns)

    shrink_flat = shrink_panels.transpose(1, 0, 2).reshape(width, per_device * rank)
    base, low = gather_and_multiply(features, qkv_weight, shrink_flat, Z, Y)

    held = jnp.arange(2)[:, None] * T * per_device + t * per_device + jnp.arange(per_device)[None, :]
    held = held.reshape(-1).astype(jnp.int32)
    low = low.reshape(rows, 2 * per_device, rank)
    low = jnp.sum(jnp.where((slot[:, None] == held[None, :])[:, :, None], low, 0), axis=1, dtype=jnp.bfloat16)
    shrunk = lax.psum(low, "tensor")
    match = slot[:, None] == jnp.arange(adapter_count, dtype=jnp.int32)[None, :]
    spread = jnp.where(match[:, :, None], shrunk[:, None, :], 0).astype(jnp.bfloat16)
    spread = spread.reshape(rows, adapter_count * rank)
    delta = jnp.dot(spread, panels, preferred_element_type=jnp.float32).astype(jnp.bfloat16)
    return (base + delta.astype(jnp.float32)).astype(jnp.bfloat16)


def solution(mesh):
    Y = max(1, 4 // mesh.shape["groups"])
    Z = mesh.shape["tensor"] // Y
    return jax.shard_map(
        functools.partial(on_device, Z, Y),
        mesh=mesh,
        in_specs=(
            P(("groups", "rows"), "tensor"),
            P(None, "tensor"),
            P(("groups", "rows"), None),
            P(),
            P(("rows", "tensor"), None, None),
            P(("rows", "tensor"), None, None),
        ),
        out_specs=P(("groups", "rows"), "tensor"),
        check_vma=False,
    )
```

```python
import functools

import jax
import jax.numpy as jnp
from jax import lax
from jax.experimental import pallas as pl
from jax.experimental.pallas import tpu as pltpu
from jax.sharding import PartitionSpec as P

CHUNKS = 8
LAG = 1


def slot_of(row_ids, owner_slot):
    count = owner_slot.shape[0]
    match = row_ids[:, None] == jnp.arange(count, dtype=jnp.int32)[None, :]
    return jnp.sum(jnp.where(match, owner_slot[None, :], 0), axis=1)


def gather_kernel(
    Z, Y, CH, NB,
    x_ref, w_ref, sh_ref, base_ref, low_ref,
    g, w, ws, acc, low,
    own_sem, w_sem, ws_sem, ws_send, ws_recv,
    up_send, dn_send, z_recv, ub_send, db_send, b_recv, y_send, y_recv, out_sem,
):
    NC = x_ref.shape[0] // CH
    DK = x_ref.shape[1]
    T = Z * Y
    NA = CH - NB
    t = lax.axis_index("tensor")
    r = lax.axis_index("rows")
    z, y = t // Y, lax.rem(t, Y)
    has_up, has_dn = z < Z - 1, z > 0
    up, dn, side = {"tensor": t + Y}, {"tensor": t - Y}, {"tensor": z * Y + (1 - y)}
    twin = {"rows": 1 - r}

    barrier = pltpu.get_barrier_semaphore()

    @pl.when(has_up)
    def _():
        pl.semaphore_signal(barrier, inc=1, device_id=up)

    @pl.when(has_dn)
    def _():
        pl.semaphore_signal(barrier, inc=1, device_id=dn)

    if Y == 2:
        pl.semaphore_signal(barrier, inc=1, device_id=side)
    pl.semaphore_signal(barrier, inc=1, device_id=twin)
    pl.semaphore_wait(barrier, has_up.astype(jnp.int32) + has_dn.astype(jnp.int32) + Y)

    own_copy = pltpu.make_async_copy(x_ref, g.at[t], own_sem)
    w_copy = pltpu.make_async_copy(w_ref, w, w_sem)
    ws_cols = pl.ds(pl.multiple_of(r * 128, 128), 128)
    ws_copy = pltpu.make_async_copy(sh_ref, ws.at[:, ws_cols], ws_sem)
    ws_remote = pltpu.make_async_remote_copy(
        src_ref=sh_ref, dst_ref=ws.at[:, ws_cols], send_sem=ws_send, recv_sem=ws_recv, device_id=twin,
    )
    twin_cols = pl.ds(pl.multiple_of((1 - r) * 128, 128), 128)
    ws_in = pltpu.make_async_remote_copy(
        src_ref=sh_ref, dst_ref=ws.at[:, twin_cols], send_sem=ws_send, recv_sem=ws_recv, device_id=twin,
    )

    def rows_all(c):
        return pl.ds(pl.multiple_of(c * CH, CH), CH)

    def rows_a(c):
        return pl.ds(pl.multiple_of(c * CH, 16), NA)

    def rows_b(c):
        return pl.ds(pl.multiple_of(c * CH + NA, 16), NB)

    def place(zs, ys, rows):
        return g.at[zs * Y + ys, rows]

    def own_src(c):
        return x_ref.at[rows_all(c)]

    def along(c, zs, src, upward):
        return pltpu.make_async_remote_copy(
            src_ref=src, dst_ref=place(zs, y, rows_all(c)),
            send_sem=(up_send if upward else dn_send).at[c, zs], recv_sem=z_recv.at[c, zs],
            device_id=up if upward else dn,
        )

    def along_b(c, zs, upward):
        ref = place(zs, 1 - y, rows_b(c))
        return pltpu.make_async_remote_copy(
            src_ref=ref, dst_ref=ref,
            send_sem=(ub_send if upward else db_send).at[c, zs], recv_sem=b_recv.at[c, zs],
            device_id=up if upward else dn,
        )

    def across_own(c):
        return pltpu.make_async_remote_copy(
            src_ref=own_src(c), dst_ref=place(z, y, rows_all(c)),
            send_sem=y_send.at[c, z], recv_sem=y_recv.at[c, z], device_id=side,
        )

    def across(c, zs):
        ref = place(zs, y, rows_a(c))
        return pltpu.make_async_remote_copy(
            src_ref=ref, dst_ref=ref,
            send_sem=y_send.at[c, zs], recv_sem=y_recv.at[c, zs], device_id=side,
        )

    def wait_into(ref, sem):
        pltpu.make_async_remote_copy(
            src_ref=ref, dst_ref=ref, send_sem=sem, recv_sem=sem, device_id=twin,
        ).wait_recv()

    def when_chunk(c, cond=True):
        return pl.when((c >= 0) & (c < NC) & cond)

    def out_copies(c):
        slot = lax.rem(c, 2)
        return (
            pltpu.make_async_copy(acc.at[slot], base_ref.at[rows_all(c)], out_sem.at[slot, 0]),
            pltpu.make_async_copy(low.at[slot], low_ref.at[rows_all(c)], out_sem.at[slot, 1]),
        )

    def compute(c):
        slot = lax.rem(c, 2)

        @pl.when(c >= 2)
        def _():
            for copy in out_copies(c - 2):
                copy.wait()

        def one(s, sums):
            rows = g[s, rows_all(c), :]
            depth = pl.ds(pl.multiple_of(s * DK, DK), DK)
            part = jnp.dot(rows, w[depth, :], preferred_element_type=jnp.float32)
            first = s == 0
            acc[slot] = jnp.where(first, part, acc[slot] + part)
            return sums + jnp.dot(rows, ws[depth, :], preferred_element_type=jnp.float32)

        sums = lax.fori_loop(0, T, one, jnp.zeros((CH, 256), jnp.float32))
        low[slot] = sums.astype(low.dtype)
        for copy in out_copies(c):
            copy.start()

    def step(k, carry):
        @pl.when(k < NC)
        def _():
            @pl.when(has_up)
            def _():
                along(k, z, own_src(k), True).start()

            @pl.when(has_dn)
            def _():
                along(k, z, own_src(k), False).start()

            if Y == 2:
                across_own(k).start()

        @pl.when(k == 0)
        def _():
            ws_remote.start()
            ws_copy.start()
            own_copy.start()
            w_copy.start()

        if Y == 2:
            c1 = k - LAG

            @when_chunk(c1)
            def _():
                wait_into(place(z, 1 - y, rows_all(c1)), y_recv.at[c1, z])

                @pl.when(has_up)
                def _():
                    along_b(c1, z, True).start()

                @pl.when(has_dn)
                def _():
                    along_b(c1, z, False).start()

        for d in range(1, Z):
            for upward in (True, False):
                zs = z - d if upward else z + d
                here = zs >= 0 if upward else zs < Z
                more = has_up if upward else has_dn
                c = k - LAG * d

                @when_chunk(c, here)
                def _(c=c, zs=zs, upward=upward, more=more):
                    ref = place(zs, y, rows_all(c))
                    wait_into(ref, z_recv.at[c, zs])

                    @pl.when(more)
                    def _():
                        along(c, zs, ref, upward).start()

                    if Y == 2:
                        across(c, zs).start()

                if Y == 2:
                    cb = k - LAG * (d + 1)

                    @when_chunk(cb, here)
                    def _(c=cb, zs=zs, upward=upward, more=more):
                        wait_into(place(zs, 1 - y, rows_b(c)), b_recv.at[c, zs])

                        @pl.when(more)
                        def _():
                            along_b(c, zs, upward).start()

        @pl.when(k == LAG * Z)
        def _():
            own_copy.wait()
            w_copy.wait()
            ws_copy.wait()
            ws_in.wait_recv()

        cc = k - LAG * Z

        @when_chunk(cc)
        def _():
            if Y == 2:
                for zs in range(Z):
                    @pl.when(zs != z)
                    def _(zs=zs):
                        wait_into(place(zs, 1 - y, rows_a(cc)), y_recv.at[cc, zs])
            compute(cc)

        return carry

    lax.fori_loop(0, NC + LAG * Z, step, 0)

    for c in range(NC - 2, NC):
        for copy in out_copies(c):
            copy.wait()

    ws_remote.wait_send()

    def drain(c, carry):
        for zs in range(Z):
            ref = place(zs, y, rows_all(c))

            @pl.when(has_up & (zs <= z))
            def _(zs=zs, ref=ref):
                along(c, zs, ref, True).wait_send()
                if Y == 2:
                    along_b(c, zs, True).wait_send()

            @pl.when(has_dn & (zs >= z))
            def _(zs=zs, ref=ref):
                along(c, zs, ref, False).wait_send()
                if Y == 2:
                    along_b(c, zs, False).wait_send()

            if Y == 2:
                @pl.when(zs == z)
                def _():
                    across_own(c).wait_send()

                @pl.when(zs != z)
                def _(zs=zs):
                    across(c, zs).wait_send()
        return carry

    lax.fori_loop(0, NC, drain, 0)


def gather_and_multiply(features, weight, shrink_flat, Z, Y):
    rows, depth = features.shape
    width, columns = weight.shape
    T = Z * Y
    CH = rows // CHUNKS
    NB = CH // 6 // 16 * 16
    DMA = pltpu.SemaphoreType.DMA
    per = (CHUNKS, Z)
    few = per if Y == 2 else (1, 1)
    return pl.pallas_call(
        functools.partial(gather_kernel, Z, Y, CH, NB),
        out_shape=(
            jax.ShapeDtypeStruct((rows, columns), jnp.float32),
            jax.ShapeDtypeStruct((rows, 256), jnp.bfloat16),
        ),
        in_specs=[pl.BlockSpec(memory_space=pl.ANY)] * 3,
        out_specs=[pl.BlockSpec(memory_space=pl.ANY)] * 2,
        scratch_shapes=[
            pltpu.VMEM((T, rows, depth), jnp.bfloat16),
            pltpu.VMEM((width, columns), jnp.bfloat16),
            pltpu.VMEM((width, 256), jnp.bfloat16),
            pltpu.VMEM((2, CH, columns), jnp.float32),
            pltpu.VMEM((2, CH, 256), jnp.bfloat16),
            DMA, DMA, DMA, DMA, DMA,
            DMA(per), DMA(per), DMA(per), DMA(few), DMA(few), DMA(few), DMA(few), DMA(few),
            DMA((2, 2)),
        ],
        compiler_params=pltpu.CompilerParams(
            collective_id=0, has_side_effects=True, vmem_limit_bytes=62 * 1024 * 1024,
        ),
        cost_estimate=pl.CostEstimate(
            flops=2 * rows * width * (columns + 256), bytes_accessed=200_000_000, transcendentals=0,
        ),
    )(features, weight, shrink_flat)


def on_device(Z, Y, features, qkv_weight, adapter_ids, owner_slot, shrink_panels, expand_panels):
    rows = features.shape[0]
    columns = qkv_weight.shape[1]
    T = Z * Y
    per_device, width, rank = shrink_panels.shape
    adapter_count = owner_slot.shape[0]
    G = lax.axis_size("groups")
    t = lax.axis_index("tensor")
    slot = slot_of(adapter_ids[:, 0], owner_slot)

    share = rank // G
    mine = lax.dynamic_slice_in_dim(expand_panels, lax.axis_index("groups") * share, share, 1)
    mine = mine.reshape(per_device, share, T, columns).transpose(2, 0, 1, 3)
    got = lax.all_to_all(mine, "tensor", split_axis=0, concat_axis=0, tiled=True)
    panels = lax.all_gather(got, ("rows", "groups"), axis=0, tiled=False)
    panels = panels.reshape(2, G, T, per_device, share, columns).transpose(0, 2, 3, 1, 4, 5)
    panels = panels.reshape(adapter_count * rank, columns)

    shrink_flat = shrink_panels.transpose(1, 0, 2).reshape(width, per_device * rank)
    base, low = gather_and_multiply(features, qkv_weight, shrink_flat, Z, Y)

    held = jnp.arange(2)[:, None] * T * per_device + t * per_device + jnp.arange(per_device)[None, :]
    held = held.reshape(-1).astype(jnp.int32)
    low = low.reshape(rows, 2 * per_device, rank)
    low = jnp.sum(jnp.where((slot[:, None] == held[None, :])[:, :, None], low, 0), axis=1, dtype=jnp.bfloat16)
    half = rows // 2
    low = jnp.concatenate([low[:half], low[half:]], axis=1).reshape(T, half // T, 2 * rank)
    terms = lax.all_to_all(low, "tensor", split_axis=0, concat_axis=0, tiled=True)
    part = jnp.sum(terms, axis=0, dtype=jnp.bfloat16)
    shrunk = lax.all_to_all(
        jnp.broadcast_to(part[None], terms.shape), "tensor", split_axis=0, concat_axis=0, tiled=True
    ).reshape(half, 2 * rank)
    shrunk = jnp.concatenate([shrunk[:, :rank], shrunk[:, rank:]], axis=0)
    match = slot[:, None] == jnp.arange(adapter_count, dtype=jnp.int32)[None, :]
    spread = jnp.where(match[:, :, None], shrunk[:, None, :], 0).astype(jnp.bfloat16)
    spread = spread.reshape(rows, adapter_count * rank)
    delta = jnp.dot(spread, panels, preferred_element_type=jnp.float32).astype(jnp.bfloat16)
    return (base + delta.astype(jnp.float32)).astype(jnp.bfloat16)


def solution(mesh):
    Y = max(1, 4 // mesh.shape["groups"])
    Z = mesh.shape["tensor"] // Y
    return jax.shard_map(
        functools.partial(on_device, Z, Y),
        mesh=mesh,
        in_specs=(
            P(("groups", "rows"), "tensor"),
            P(None, "tensor"),
            P(("groups", "rows"), None),
            P(),
            P(("rows", "tensor"), None, None),
            P(("rows", "tensor"), None, None),
        ),
        out_specs=P(("groups", "rows"), "tensor"),
        check_vma=False,
    )
```

```python
import functools

import jax
import jax.numpy as jnp
from jax import lax
from jax.experimental import pallas as pl
from jax.experimental.pallas import tpu as pltpu
from jax.sharding import PartitionSpec as P

CHUNKS = 8
LAG = 1


def slot_of(row_ids, owner_slot):
    count = owner_slot.shape[0]
    match = row_ids[:, None] == jnp.arange(count, dtype=jnp.int32)[None, :]
    return jnp.sum(jnp.where(match, owner_slot[None, :], 0), axis=1)


def gather_kernel(
    Z, Y, G, CH, NB,
    x_ref, w_ref, sh_ref, cut_ref, base_ref, low_ref, e_ref,
    g, w, ws, acc, low,
    e_sem, e_send, e_recv, p_send, p_recv,
    own_sem, w_sem, ws_sem, ws_send, ws_recv,
    up_send, dn_send, z_recv, ub_send, db_send, b_recv, y_send, y_recv, out_sem,
):
    NC = x_ref.shape[0] // CH
    DK = x_ref.shape[1]
    T = Z * Y
    NA = CH - NB
    t = lax.axis_index("tensor")
    r = lax.axis_index("rows")
    z, y = t // Y, lax.rem(t, Y)
    has_up, has_dn = z < Z - 1, z > 0
    up, dn, side = {"tensor": t + Y}, {"tensor": t - Y}, {"tensor": z * Y + (1 - y)}
    twin = {"rows": 1 - r}

    barrier = pltpu.get_barrier_semaphore()

    for d in range(1, T):
        pl.semaphore_signal(barrier, inc=1, device_id={"tensor": lax.rem(t + d, T)})
    peers = 2 * G
    group = lax.axis_index("groups")
    at = r * G + group

    def peer(e):
        p = lax.rem(at + e, peers)
        return {"rows": p // G, "groups": lax.rem(p, G)}

    for e in range(1, peers):
        pl.semaphore_signal(barrier, inc=1, device_id=peer(e))
    pl.semaphore_wait(barrier, T - 1 + peers - 1)

    e_own = pltpu.make_async_copy(cut_ref.at[t], e_ref.at[at, t], e_sem)

    def e_out(d):
        to = lax.rem(t + d, T)
        return pltpu.make_async_remote_copy(
            src_ref=cut_ref.at[to], dst_ref=e_ref.at[at, t],
            send_sem=e_send.at[d], recv_sem=e_recv.at[d], device_id={"tensor": to},
        )

    def e_in(d):
        return pltpu.make_async_remote_copy(
            src_ref=cut_ref.at[t], dst_ref=e_ref.at[at, lax.rem(t + T - d, T)],
            send_sem=e_send.at[d], recv_sem=e_recv.at[d], device_id={"tensor": lax.rem(t + d, T)},
        )

    def p_out(e):
        return pltpu.make_async_remote_copy(
            src_ref=e_ref.at[at], dst_ref=e_ref.at[at],
            send_sem=p_send.at[e], recv_sem=p_recv.at[e], device_id=peer(e),
        )

    def p_in(e):
        ref = e_ref.at[lax.rem(at + peers - e, peers)]
        return pltpu.make_async_remote_copy(
            src_ref=ref, dst_ref=ref,
            send_sem=p_send.at[e], recv_sem=p_recv.at[e], device_id=peer(e),
        )

    own_copy = pltpu.make_async_copy(x_ref, g.at[t], own_sem)
    w_copy = pltpu.make_async_copy(w_ref, w, w_sem)
    ws_cols = pl.ds(pl.multiple_of(r * 128, 128), 128)
    ws_copy = pltpu.make_async_copy(sh_ref, ws.at[:, ws_cols], ws_sem)
    ws_remote = pltpu.make_async_remote_copy(
        src_ref=sh_ref, dst_ref=ws.at[:, ws_cols], send_sem=ws_send, recv_sem=ws_recv, device_id=twin,
    )
    twin_cols = pl.ds(pl.multiple_of((1 - r) * 128, 128), 128)
    ws_in = pltpu.make_async_remote_copy(
        src_ref=sh_ref, dst_ref=ws.at[:, twin_cols], send_sem=ws_send, recv_sem=ws_recv, device_id=twin,
    )

    def rows_all(c):
        return pl.ds(pl.multiple_of(c * CH, CH), CH)

    def rows_a(c):
        return pl.ds(pl.multiple_of(c * CH, 16), NA)

    def rows_b(c):
        return pl.ds(pl.multiple_of(c * CH + NA, 16), NB)

    def place(zs, ys, rows):
        return g.at[zs * Y + ys, rows]

    def own_src(c):
        return x_ref.at[rows_all(c)]

    def along(c, zs, src, upward):
        return pltpu.make_async_remote_copy(
            src_ref=src, dst_ref=place(zs, y, rows_all(c)),
            send_sem=(up_send if upward else dn_send).at[c, zs], recv_sem=z_recv.at[c, zs],
            device_id=up if upward else dn,
        )

    def along_b(c, zs, upward):
        ref = place(zs, 1 - y, rows_b(c))
        return pltpu.make_async_remote_copy(
            src_ref=ref, dst_ref=ref,
            send_sem=(ub_send if upward else db_send).at[c, zs], recv_sem=b_recv.at[c, zs],
            device_id=up if upward else dn,
        )

    def across_own(c):
        return pltpu.make_async_remote_copy(
            src_ref=own_src(c), dst_ref=place(z, y, rows_all(c)),
            send_sem=y_send.at[c, z], recv_sem=y_recv.at[c, z], device_id=side,
        )

    def across(c, zs):
        ref = place(zs, y, rows_a(c))
        return pltpu.make_async_remote_copy(
            src_ref=ref, dst_ref=ref,
            send_sem=y_send.at[c, zs], recv_sem=y_recv.at[c, zs], device_id=side,
        )

    def wait_into(ref, sem):
        pltpu.make_async_remote_copy(
            src_ref=ref, dst_ref=ref, send_sem=sem, recv_sem=sem, device_id=twin,
        ).wait_recv()

    def when_chunk(c, cond=True):
        return pl.when((c >= 0) & (c < NC) & cond)

    def out_copies(c):
        slot = lax.rem(c, 2)
        return (
            pltpu.make_async_copy(acc.at[slot], base_ref.at[rows_all(c)], out_sem.at[slot, 0]),
            pltpu.make_async_copy(low.at[slot], low_ref.at[rows_all(c)], out_sem.at[slot, 1]),
        )

    def compute(c):
        slot = lax.rem(c, 2)

        @pl.when(c >= 2)
        def _():
            for copy in out_copies(c - 2):
                copy.wait()

        def one(s, sums):
            rows = g[s, rows_all(c), :]
            depth = pl.ds(pl.multiple_of(s * DK, DK), DK)
            part = jnp.dot(rows, w[depth, :], preferred_element_type=jnp.float32)
            first = s == 0
            acc[slot] = jnp.where(first, part, acc[slot] + part)
            return sums + jnp.dot(rows, ws[depth, :], preferred_element_type=jnp.float32)

        sums = lax.fori_loop(0, T, one, jnp.zeros((CH, 256), jnp.float32))
        low[slot] = sums.astype(low.dtype)
        for copy in out_copies(c):
            copy.start()

    def step(k, carry):
        @pl.when(k < NC)
        def _():
            @pl.when(has_up)
            def _():
                along(k, z, own_src(k), True).start()

            @pl.when(has_dn)
            def _():
                along(k, z, own_src(k), False).start()

            if Y == 2:
                across_own(k).start()

        @pl.when(k == 0)
        def _():
            ws_remote.start()
            ws_copy.start()
            own_copy.start()
            w_copy.start()
            e_own.start()
            for d in range(1, T):
                e_out(d).start()

        @pl.when(k == Z)
        def _():
            e_own.wait()
            for d in range(1, T):
                e_in(d).wait_recv()
            for e in range(1, peers):
                p_out(e).start()

        if Y == 2:
            c1 = k - LAG

            @when_chunk(c1)
            def _():
                wait_into(place(z, 1 - y, rows_all(c1)), y_recv.at[c1, z])

                @pl.when(has_up)
                def _():
                    along_b(c1, z, True).start()

                @pl.when(has_dn)
                def _():
                    along_b(c1, z, False).start()

        for d in range(1, Z):
            for upward in (True, False):
                zs = z - d if upward else z + d
                here = zs >= 0 if upward else zs < Z
                more = has_up if upward else has_dn
                c = k - LAG * d

                @when_chunk(c, here)
                def _(c=c, zs=zs, upward=upward, more=more):
                    ref = place(zs, y, rows_all(c))
                    wait_into(ref, z_recv.at[c, zs])

                    @pl.when(more)
                    def _():
                        along(c, zs, ref, upward).start()

                    if Y == 2:
                        across(c, zs).start()

                if Y == 2:
                    cb = k - LAG * (d + 1)

                    @when_chunk(cb, here)
                    def _(c=cb, zs=zs, upward=upward, more=more):
                        wait_into(place(zs, 1 - y, rows_b(c)), b_recv.at[c, zs])

                        @pl.when(more)
                        def _():
                            along_b(c, zs, upward).start()

        @pl.when(k == LAG * Z)
        def _():
            own_copy.wait()
            w_copy.wait()
            ws_copy.wait()
            ws_in.wait_recv()

        cc = k - LAG * Z

        @when_chunk(cc)
        def _():
            if Y == 2:
                for zs in range(Z):
                    @pl.when(zs != z)
                    def _(zs=zs):
                        wait_into(place(zs, 1 - y, rows_a(cc)), y_recv.at[cc, zs])
            compute(cc)

        return carry

    lax.fori_loop(0, NC + LAG * Z, step, 0)

    for c in range(NC - 2, NC):
        for copy in out_copies(c):
            copy.wait()

    ws_remote.wait_send()
    for d in range(1, T):
        e_out(d).wait_send()
    for e in range(1, peers):
        p_out(e).wait_send()
        p_in(e).wait_recv()

    def drain(c, carry):
        for zs in range(Z):
            ref = place(zs, y, rows_all(c))

            @pl.when(has_up & (zs <= z))
            def _(zs=zs, ref=ref):
                along(c, zs, ref, True).wait_send()
                if Y == 2:
                    along_b(c, zs, True).wait_send()

            @pl.when(has_dn & (zs >= z))
            def _(zs=zs, ref=ref):
                along(c, zs, ref, False).wait_send()
                if Y == 2:
                    along_b(c, zs, False).wait_send()

            if Y == 2:
                @pl.when(zs == z)
                def _():
                    across_own(c).wait_send()

                @pl.when(zs != z)
                def _(zs=zs):
                    across(c, zs).wait_send()
        return carry

    lax.fori_loop(0, NC, drain, 0)


def gather_and_multiply(features, weight, shrink_flat, cut, Z, Y, G):
    rows, depth = features.shape
    width, columns = weight.shape
    T = Z * Y
    CH = rows // CHUNKS
    NB = CH // 6 // 16 * 16
    DMA = pltpu.SemaphoreType.DMA
    per = (CHUNKS, Z)
    few = per if Y == 2 else (1, 1)
    return pl.pallas_call(
        functools.partial(gather_kernel, Z, Y, G, CH, NB),
        out_shape=(
            jax.ShapeDtypeStruct((rows, columns), jnp.float32),
            jax.ShapeDtypeStruct((rows, 256), jnp.bfloat16),
            jax.ShapeDtypeStruct((2 * G,) + cut.shape, jnp.bfloat16),
        ),
        in_specs=[pl.BlockSpec(memory_space=pl.ANY)] * 4,
        out_specs=[pl.BlockSpec(memory_space=pl.ANY)] * 3,
        scratch_shapes=[
            pltpu.VMEM((T, rows, depth), jnp.bfloat16),
            pltpu.VMEM((width, columns), jnp.bfloat16),
            pltpu.VMEM((width, 256), jnp.bfloat16),
            pltpu.VMEM((2, CH, columns), jnp.float32),
            pltpu.VMEM((2, CH, 256), jnp.bfloat16),
            DMA, DMA((T,)), DMA((T,)), DMA((2 * G,)), DMA((2 * G,)),
            DMA, DMA, DMA, DMA, DMA,
            DMA(per), DMA(per), DMA(per), DMA(few), DMA(few), DMA(few), DMA(few), DMA(few),
            DMA((2, 2)),
        ],
        compiler_params=pltpu.CompilerParams(
            collective_id=0, has_side_effects=True, vmem_limit_bytes=62 * 1024 * 1024,
        ),
        cost_estimate=pl.CostEstimate(
            flops=2 * rows * width * (columns + 256), bytes_accessed=200_000_000, transcendentals=0,
        ),
    )(features, weight, shrink_flat, cut)


def on_device(Z, Y, features, qkv_weight, adapter_ids, owner_slot, shrink_panels, expand_panels):
    rows = features.shape[0]
    columns = qkv_weight.shape[1]
    T = Z * Y
    per_device, width, rank = shrink_panels.shape
    adapter_count = owner_slot.shape[0]
    G = lax.axis_size("groups")
    t = lax.axis_index("tensor")
    slot = slot_of(adapter_ids[:, 0], owner_slot)

    share = rank // G
    mine = lax.dynamic_slice_in_dim(expand_panels, lax.axis_index("groups") * share, share, 1)
    cut = mine.reshape(per_device * share, T, columns).transpose(1, 0, 2)
    shrink_flat = shrink_panels.transpose(1, 0, 2).reshape(width, per_device * rank)
    base, low, panels = gather_and_multiply(features, qkv_weight, shrink_flat, cut, Z, Y, G)
    panels = panels.reshape(adapter_count * rank, columns)

    held = jnp.arange(2)[:, None] * T * per_device + t * per_device + jnp.arange(per_device)[None, :]
    held = held.reshape(-1).astype(jnp.int32)
    low = low.reshape(rows, 2 * per_device, rank)
    low = jnp.sum(jnp.where((slot[:, None] == held[None, :])[:, :, None], low, 0), axis=1, dtype=jnp.bfloat16)
    half = rows // 2
    low = jnp.concatenate([low[:half], low[half:]], axis=1).reshape(T, half // T, 2 * rank)
    terms = lax.all_to_all(low, "tensor", split_axis=0, concat_axis=0, tiled=True)
    part = jnp.sum(terms, axis=0, dtype=jnp.bfloat16)
    shrunk = lax.all_to_all(
        jnp.broadcast_to(part[None], terms.shape), "tensor", split_axis=0, concat_axis=0, tiled=True
    ).reshape(half, 2 * rank)
    shrunk = jnp.concatenate([shrunk[:, :rank], shrunk[:, rank:]], axis=0)
    match = (slot[:, None] == jnp.arange(adapter_count, dtype=jnp.int32)[None, :])
    match = match.reshape(rows, 2, 1, T * per_device, 1)
    spread = jnp.where(match, shrunk.reshape(rows, 1, G, 1, share), 0).astype(jnp.bfloat16)
    spread = spread.reshape(rows, adapter_count * rank)
    delta = jnp.dot(spread, panels, preferred_element_type=jnp.float32).astype(jnp.bfloat16)
    return (base + delta.astype(jnp.float32)).astype(jnp.bfloat16)


def solution(mesh):
    Y = max(1, 4 // mesh.shape["groups"])
    Z = mesh.shape["tensor"] // Y
    return jax.shard_map(
        functools.partial(on_device, Z, Y),
        mesh=mesh,
        in_specs=(
            P(("groups", "rows"), "tensor"),
            P(None, "tensor"),
            P(("groups", "rows"), None),
            P(),
            P(("rows", "tensor"), None, None),
            P(("rows", "tensor"), None, None),
        ),
        out_specs=P(("groups", "rows"), "tensor"),
        check_vma=False,
    )
```
